256 devices in a mesh: depth: 16 (over z, core), image: 16 (over x, y).
Axes of the slice: x: 4, y: 4, z: 8, core: 2. Of those that a mesh axis runs over, the one named last changes fastest.
Arguments:
- level_set: float32 [256, 1024, 512], P('depth', 'image'), may hold values from -6 to 6
- velocity: float32 [3, 256, 1024, 512], P(None, 'depth', 'image'), may hold values from -1 to 1
- view_flag: int32 [16], replicated, may hold values from 0 to 1
- slab_rank: int32 [16], replicated, may hold values from 0 to 15, each once
Outputs:
- image_first: float32 [4, 1024, 512], P(None, 'image', 'depth')
- image_second: float32 [4, 1024, 512], P(None, 'image', 'depth')
- level_next: float32 [256, 1024, 512], P('depth', 'image')
The draws below stay inside these ranges and needn't reach their ends.
Inputs may be any that keep to these rules, and one draw needn't show every extreme that they name: `slab_rank`: each of 0 to 15 once.
All inputs are finite; a program needn't handle non-finite values.
Results may differ from the reference program's by a relative error of at most 0.00013.
Values sent between devices are 32-bit elements; how exact they have to be, the bound alone decides.
A program may use at most 64 MiB of HBM per device.

```python
import jax
import jax.numpy as jnp
from jax import lax

CZ = 16
STEPS = 4
NZ = 256
NX = 1024
NY = 512
N_DEPTH = 16


def plant(entries, stream_key, least, high):
    spot = [jax.random.randint(jax.random.fold_in(stream_key, axis), (), 0, length) for axis, length in enumerate(entries.shape)]
    main_axis = entries.shape.index(max(entries.shape))
    neighbour = spot[:main_axis] + [(spot[main_axis] + 1) % entries.shape[main_axis]] + spot[main_axis + 1:]
    return entries.at[tuple(spot)].set(least).at[tuple(neighbour)].set(high)


def levels(rng, extent, pieces, low, top_value):
    level, own = 1.0, jax.random.fold_in(rng, 6)
    for dim, shards_of in pieces:
        draws = jnp.exp(jax.random.uniform(jax.random.fold_in(own, dim), (shards_of,), jnp.float32, low / len(pieces), top_value / len(pieces)))
        level = level * jnp.repeat(draws, extent[dim] // shards_of).reshape([-1 if axis == dim else 1 for axis in range(len(extent))])
    return level


def scatter_about(key, extent, scale, most, cuts=(), held_as=jnp.bfloat16):
    factor_of = levels(key, extent, cuts, -0.22, 0.18) if cuts else 1.0
    array = jax.random.normal(key, extent, jnp.float32) * scale * factor_of
    return jnp.minimum(jnp.maximum(array, -most), most).astype(held_as)


def setup_inputs(seed: int = 0) -> dict:
    seeds = jax.random.split(jax.random.key(seed), 5)
    return {
        "level_set": scatter_about(seeds[0], (NZ, NX, NY), 1.0, 6.0, ((0, 16), (1, 16)), jnp.float32),
        "velocity": jnp.clip(jax.random.uniform(seeds[1], (3, NZ, NX, NY), jnp.float32, -1.0, 1.0) * levels(seeds[1], (3, NZ, NX, NY), ((1, 16), (2, 16)), -0.4, 0.0), -1.0, 1.0),
        "view_flag": plant(jax.random.randint(seeds[2], (N_DEPTH,), 0, 2), jax.random.fold_in(seeds[2], 1), 0, 1).astype(jnp.int32),
        "slab_rank": jax.random.permutation(seeds[3], N_DEPTH).astype(jnp.int32),
    }


step_size = 0.3


def upwind(padded):
    center = padded[1:-1, 1:-1, 1:-1]
    lows = (padded[:-2, 1:-1, 1:-1], padded[1:-1, :-2, 1:-1], padded[1:-1, 1:-1, :-2])
    highs = (padded[2:, 1:-1, 1:-1], padded[1:-1, 2:, 1:-1], padded[1:-1, 1:-1, 2:])
    return center, lows, highs


def advect(center, lows, highs, velocity):
    rate = jnp.zeros_like(center)
    for k in range(3):
        speed = velocity[k]
        rate = rate + jnp.maximum(speed, 0.0) * (center - lows[k]) + jnp.minimum(speed, 0.0) * (highs[k] - center)
    return center - step_size * rate


def render_slabs(field, flags, scale):
    density = scale * jnp.exp(-field * field)
    colour = jnp.stack([jax.nn.sigmoid(2.0 * field), jnp.exp(-field * field), jax.nn.sigmoid(-2.0 * field)], axis=-4)
    running = jnp.cumsum(density, axis=-3)
    totals = running[..., -1:, :, :]
    before = jnp.where(flags[:, None, None, None] == 0, running - density, totals - running)
    weight = jnp.exp(-before) * (1.0 - jnp.exp(-density))
    partial_colour = jnp.sum(weight[..., None, :, :, :] * colour, axis=-3)
    return partial_colour, -totals[..., 0, :, :]


def composite(partial_colour, log_trans, slab_rank):
    earlier_mask = (slab_rank[None, :] < slab_rank[:, None]).astype(jnp.float32)
    earlier = jnp.einsum('de,exy->dxy', earlier_mask, log_trans, precision=lax.Precision.HIGHEST)
    rgb = jnp.sum(jnp.exp(earlier)[:, None] * partial_colour, axis=0)
    alpha = 1.0 - jnp.exp(jnp.sum(log_trans, axis=0))
    return jnp.concatenate([rgb, alpha[None]], axis=0)


def frame_image(field, view_flag, slab_rank):
    slabs = field.reshape(N_DEPTH, CZ, NX, NY)
    partial_colour, log_trans = render_slabs(slabs, view_flag, 2.0 / NZ)
    return composite(partial_colour, log_trans, slab_rank)


def reference(level_set, velocity, view_flag, slab_rank):
    image_first = frame_image(level_set, view_flag, slab_rank)
    field = level_set
    for step in range(STEPS):
        center, lows, highs = upwind(jnp.pad(field, 1))
        field = advect(center, lows, highs, velocity)
    image_second = frame_image(field, view_flag, slab_rank)
    return image_first, image_second, field
```

```python
import functools

import jax
import jax.numpy as jnp
from jax import lax
from jax.experimental import pallas as pl
from jax.experimental.pallas import tpu as pltpu
from jax.sharding import PartitionSpec as P

STEPS = 4
DT = 0.3
CHUNKS = 4
MESH = pl.DeviceIdType.MESH


def kernel(dims, plan_hbm, field_hbm, speed_hbm, image_a, image_b, lev_4,
           lev_0, lev_1, lev_2, lev_3, plan_ref, vel, zh, xh, xsnd, pk, rc_a, rc_b, order, load_sem, zs, zr, xs, xr, ss, rs, own_sem):
    slabs, images, layers, rows, cols = dims
    tiles, pieces = rows // 8, cols // 128
    width = cols // slabs
    per = 128 // width
    chunk_rows = rows // CHUNKS
    scale = 2.0 / (layers * slabs)
    d = lax.axis_index("depth")
    i = lax.axis_index("image")
    d_up, d_dn = lax.rem(d + 1, slabs), lax.rem(d + slabs - 1, slabs)
    i_up, i_dn = lax.rem(i + 1, images), lax.rem(i + images - 1, images)

    rc = (rc_a, rc_b)
    fld = (lev_0, lev_1, lev_2, lev_3, lev_4)

    barrier = pltpu.get_barrier_semaphore()

    @pl.loop(1, slabs)
    def _(k):
        pl.semaphore_signal(barrier, inc=1, device_id={"depth": lax.rem(d + k, slabs)}, device_id_type=MESH)

    for other in (i_up, i_dn):
        pl.semaphore_signal(barrier, inc=1, device_id={"image": other}, device_id_type=MESH)

    load_field = pltpu.make_async_copy(field_hbm, fld[0], load_sem.at[0])
    load_speed = pltpu.make_async_copy(speed_hbm, vel, load_sem.at[1])
    load_plan = pltpu.make_async_copy(plan_hbm, plan_ref, load_sem.at[2])
    load_field.start()
    load_plan.start()
    load_speed.start()

    lane = lax.broadcasted_iota(jnp.int32, (8, 128), 1)
    sub = lax.broadcasted_iota(jnp.int32, (8, 128), 0)
    block = lane // width

    def z_copies(s):
        return (
            pltpu.make_async_remote_copy(fld[s].at[layers - 1], zh.at[0, s], zs.at[0, s], zr.at[0, s],
                                         device_id={"depth": d_up}, device_id_type=MESH),
            pltpu.make_async_remote_copy(fld[s].at[0], zh.at[1, s], zs.at[1, s], zr.at[1, s],
                                         device_id={"depth": d_dn}, device_id_type=MESH),
        )

    def x_copies(s):
        return (
            pltpu.make_async_remote_copy(xsnd.at[0, s], xh.at[0, s], xs.at[0, s], xr.at[0, s],
                                         device_id={"image": i_up}, device_id_type=MESH),
            pltpu.make_async_remote_copy(xsnd.at[1, s], xh.at[1, s], xs.at[1, s], xr.at[1, s],
                                         device_id={"image": i_dn}, device_id_type=MESH),
        )

    def wait_halos(s):
        for copy in z_copies(s) + x_copies(s):
            copy.wait_recv()

        @pl.when(d == 0)
        def _():
            zh[0, s] = jnp.zeros((rows, cols), jnp.float32)

        @pl.when(d == slabs - 1)
        def _():
            zh[1, s] = jnp.zeros((rows, cols), jnp.float32)

        @pl.when(i == 0)
        def _():
            xh[0, s] = jnp.zeros((layers, 1, cols), jnp.float32)

        @pl.when(i == images - 1)
        def _():
            xh[1, s] = jnp.zeros((layers, 1, cols), jnp.float32)

    def row(f, ch):
        if isinstance(ch, int):
            return pl.ds(ch * chunk_rows, chunk_rows)
        return pl.ds(pl.multiple_of(ch * chunk_rows, chunk_rows), chunk_rows)

    def hop(n):
        return jnp.where(lax.rem(n, 2) == 0, n // 2 + 1, slabs - (n + 1) // 2)

    def send_chunk(f, ch):
        pltpu.make_async_copy(pk.at[f, d, row(f, ch)], rc[f].at[d, row(f, ch)], own_sem.at[f, ch]).start()

        @pl.loop(0, slabs - 1)
        def _(n):
            k = hop(n)
            to = lax.rem(d + k, slabs)
            pltpu.make_async_remote_copy(pk.at[f, to, row(f, ch)], rc[f].at[d, row(f, ch)], ss.at[f, ch, k], rs.at[f, ch, k],
                                         device_id={"depth": to}, device_id_type=MESH).start()

    def chunk_copy(f, ch, k):
        to, source = lax.rem(d + k, slabs), lax.rem(d + slabs - k, slabs)
        return pltpu.make_async_remote_copy(pk.at[f, to, row(f, ch)], rc[f].at[source, row(f, ch)], ss.at[f, ch, k], rs.at[f, ch, k],
                                            device_id={"depth": to}, device_id_type=MESH)

    def wait_chunk(f, ch):
        pltpu.make_async_copy(pk.at[f, d, row(f, ch)], rc[f].at[d, row(f, ch)], own_sem.at[f, ch]).wait()

        @pl.loop(1, slabs)
        def _(k):
            chunk_copy(f, ch, k).wait_recv()

    def tile_rows(t):
        if isinstance(t, int):
            return pl.ds(t * 8, 8)
        return pl.ds(pl.multiple_of(t * 8, 8), 8)

    def advance(s, z, t, z_lo, z_hi, x_lo, x_hi):
        here = tile_rows(t)
        centers = [fld[s][z, here, pl.ds(j * 128, 128)] for j in range(pieces)]
        right = [pltpu.roll(c, 1, 1) for c in centers]
        left = [pltpu.roll(c, 127, 1) for c in centers]
        zero = jnp.zeros((8, 128), jnp.float32)
        made = []
        for j in range(pieces):
            col = pl.ds(j * 128, 128)
            c = centers[j]
            y_lo = jnp.where(lane == 0, right[j - 1] if j > 0 else zero, right[j])
            y_hi = jnp.where(lane == 127, left[j + 1] if j < pieces - 1 else zero, left[j])
            low = z_lo(here, col)
            high = z_hi(here, col)
            if x_lo is None:
                x_low = pltpu.roll(jnp.where(sub == 7, fld[s][z, tile_rows(t - 1), col], c), 1, 0)
            else:
                x_low = jnp.where(sub == 0, x_lo(col), pltpu.roll(c, 1, 0))
            if x_hi is None:
                x_high = pltpu.roll(jnp.where(sub == 0, fld[s][z, tile_rows(t + 1), col], c), 7, 0)
            else:
                x_high = jnp.where(sub == 7, x_hi(col), pltpu.roll(c, 7, 0))
            rate = None
            for k, (lo, hi) in enumerate(((low, high), (x_low, x_high), (y_lo, y_hi))):
                u = vel[k, z, here, col]
                term = jnp.abs(u) * (c - jnp.where(u > 0.0, lo, hi))
                rate = term if rate is None else rate + term
            new = c - DT * rate
            fld[s + 1][z, here, col] = new
            made.append(new)
        return made

    def neighbours(s, z, kind):
        z_lo = (lambda r, c: zh[0, s, r, c]) if kind == "first" else (lambda r, c: fld[s][z - 1, r, c])
        z_hi = (lambda r, c: zh[1, s, r, c]) if kind == "last" else (lambda r, c: fld[s][z + 1, r, c])
        return z_lo, z_hi

    def keep_rows(s, z, made, side):
        for j in range(pieces):
            edge = made[j][7:8] if side == 0 else made[j][0:1]
            xsnd[side, s, z, :, pl.ds(j * 128, 128)] = edge

    def edge_tiles(s, z, kind):
        z_lo, z_hi = neighbours(s, z, kind)
        low = advance(s, z, 0, z_lo, z_hi, lambda c: xh[0, s, z, :, c], None)
        high = advance(s, z, tiles - 1, z_lo, z_hi, None, lambda c: xh[1, s, z, :, c])
        return low, high

    def layer(s, z, kind, keep):
        low, high = edge_tiles(s, z, kind)
        if keep:
            keep_rows(s + 1, z, low, 1)
            keep_rows(s + 1, z, high, 0)
        z_lo, z_hi = neighbours(s, z, kind)

        for t in range(1, tiles - 1):
            advance(s, z, t, z_lo, z_hi, None, None)

    def sides(s, keep):
        @pl.loop(0, layers // 2 - 1)
        def _(pair):
            for z in (1 + 2 * pair, 2 + 2 * pair):
                low, high = edge_tiles(s, z, "inner")
                if keep:
                    keep_rows(s + 1, z, low, 1)
                    keep_rows(s + 1, z, high, 0)

    def interior(s):
        @pl.loop(1, layers - 1)
        def _(z):
            z_lo, z_hi = neighbours(s, z, "inner")

            for t in range(1, tiles - 1):
                advance(s, z, t, z_lo, z_hi, None, None)

    def render_tile(s, f, t):
        flag = plan_ref[d]
        here = tile_rows(t)
        one, zero = jnp.ones((8, 128), jnp.float32), jnp.zeros((8, 128), jnp.float32)

        def group(g, carry):
            carry = [list(c) for c in carry]
            for q in range(4):
                n = g * 4 + q
                z = jnp.where(flag == 0, n, layers - 1 - n)
                for j in range(pieces):
                    through, odd, green, total = carry[j]
                    x = fld[s][z, here, pl.ds(j * 128, 128)]
                    bell = jnp.exp(-(x * x))
                    density = scale * bell
                    weight = through * (1.0 - jnp.exp(-density))
                    carry[j] = [through - weight, odd + weight * jnp.tanh(x), green + weight * bell, total + density]
            return tuple(tuple(c) for c in carry)

        carry = lax.fori_loop(0, layers // 4, group, tuple((one, zero, zero, zero) for _ in range(pieces)))
        for j in range(pieces):
            through, odd, green, total = carry[j]
            seen = 1.0 - through
            channels = [0.5 * (seen + odd), green, 0.5 * (seen - odd), -total]
            turned = []
            for k in range(per):
                mixed = channels[k % per]
                for q in range(1, per):
                    mixed = jnp.where(block == q, channels[(q + k) % per], mixed)
                turned.append(pltpu.roll(mixed, width * k, 1) if k else mixed)
            for q in range(per):
                packed = turned[(-q) % per]
                for c in range(1, per):
                    packed = jnp.where(block == c, turned[(c - q) % per], packed)
                pk[f, per * j + q, here, :] = packed

    def composite(f, image):
        slots = [order[r] for r in range(slabs)]

        @pl.loop(0, 2)
        def _(half):
            for q in range(tiles // 2):
                here = tile_rows(half * (tiles // 2) + q)
                total = jnp.zeros((8, 128), jnp.float32)
                colour = jnp.zeros((8, 128), jnp.float32)
                for r in range(slabs):
                    part = rc[f][slots[r], here, :]
                    log = jnp.where(block == per - 1, part, 0.0)
                    log = log + pltpu.roll(log, width, 1)
                    log = log + pltpu.roll(log, 2 * width, 1)
                    colour = colour + jnp.exp(total) * part
                    total = total + log
                image[here, :] = jnp.where(block == per - 1, 1.0 - jnp.exp(total), colour)

    load_field.wait()
    load_plan.wait()

    @pl.loop(0, layers)
    def _(z):
        for j in range(pieces):
            col = pl.ds(j * 128, 128)
            xsnd[0, 0, z, :, col] = fld[0][z, pl.ds(rows - 8, 8), col][7:8]
            xsnd[1, 0, z, :, col] = fld[0][z, pl.ds(0, 8), col][0:1]

    pl.semaphore_wait(barrier, slabs + 1)
    for copy in z_copies(0) + x_copies(0):
        copy.start()

    @pl.loop(0, tiles)
    def _(t):
        render_tile(0, 0, t)

    send_chunk(0, 0)
    ranks = [plan_ref[slabs + b] for b in range(slabs)]
    for r in range(slabs):
        found = jnp.int32(0)
        for b in range(1, slabs):
            found = jnp.where(ranks[b] == r, b, found)
        order[r] = found
    load_speed.wait()

    for s in range(STEPS - 1):
        wait_halos(s)
        layer(s, 0, "first", True)
        z_copies(s + 1)[1].start()
        layer(s, layers - 1, "last", True)
        z_copies(s + 1)[0].start()
        sides(s, True)
        for copy in x_copies(s + 1):
            copy.start()
        send_chunk(0, s + 1)
        interior(s)

    last = STEPS - 1
    interior(last)
    wait_halos(last)
    layer(last, 0, "first", False)
    layer(last, layers - 1, "last", False)
    sides(last, False)

    @pl.loop(0, CHUNKS)
    def _(ch):
        @pl.loop(0, tiles // CHUNKS)
        def _(t):
            render_tile(STEPS, 1, ch * (tiles // CHUNKS) + t)

        send_chunk(1, ch)

    @pl.loop(0, CHUNKS)
    def _(ch):
        wait_chunk(0, ch)

    composite(0, image_a)

    @pl.loop(0, CHUNKS)
    def _(ch):
        wait_chunk(1, ch)

    composite(1, image_b)

    for s in range(STEPS):
        for copy in z_copies(s) + x_copies(s):
            copy.wait_send()

    @pl.loop(0, CHUNKS)
    def _(ch):
        for f in range(2):
            @pl.loop(1, slabs)
            def _(k):
                chunk_copy(f, ch, k).wait_send()


def finish(image_a, image_b, field, first, second, next_hbm, sem):
    copy = pltpu.make_async_copy(field, next_hbm, sem)
    copy.start()
    for image, out in ((image_a, first), (image_b, second)):
        turned = image[...].T
        width = out.shape[1]
        for c in range(out.shape[0]):
            out[c] = turned[c * width:(c + 1) * width]
    copy.wait()


def local(dims, level_set, velocity, view_flag, slab_rank):
    slabs, images, layers, rows, cols = dims
    f32 = jnp.float32
    dma = pltpu.SemaphoreType.DMA
    cells = layers * rows * cols
    level = jax.ShapeDtypeStruct((layers, rows, cols), f32)
    packed = jax.ShapeDtypeStruct((rows, 128), f32)
    near = pl.BlockSpec(memory_space=pltpu.VMEM)
    far = pl.BlockSpec(memory_space=pltpu.HBM)
    parts = pl.pallas_call(
        functools.partial(kernel, dims),
        out_shape=(packed, packed, level),
        in_specs=[far] * 3,
        out_specs=(near, near, near),
        scratch_shapes=[pltpu.VMEM((layers, rows, cols), f32)] * 4 + [
            pltpu.SMEM((2 * slabs,), jnp.int32),
            pltpu.VMEM((3, layers, rows, cols), f32),
            pltpu.VMEM((2, STEPS, rows, cols), f32),
            pltpu.VMEM((2, STEPS, layers, 1, cols), f32),
            pltpu.VMEM((2, STEPS, layers, 1, cols), f32),
            pltpu.VMEM((2, slabs, rows, 128), f32),
            pltpu.VMEM((slabs, rows, 128), f32),
            pltpu.VMEM((slabs, rows, 128), f32),
            pltpu.SMEM((slabs,), jnp.int32),
            dma((3,)),
            dma((2, STEPS)),
            dma((2, STEPS)),
            dma((2, STEPS)),
            dma((2, STEPS)),
            dma((2, CHUNKS, slabs)),
            dma((2, CHUNKS, slabs)),
            dma((2, CHUNKS)),
        ],
        compiler_params=pltpu.CompilerParams(collective_id=0, has_side_effects=True, vmem_limit_bytes=51 * 1024 * 1024),
        cost_estimate=pl.CostEstimate(flops=1000000 * cells, bytes_accessed=0 * cells, transcendentals=6 * cells),
    )(jnp.concatenate([view_flag, slab_rank]), level_set, velocity)
    picture = jax.ShapeDtypeStruct((4, cols // slabs, rows), f32)
    first, second, field = pl.pallas_call(
        finish,
        out_shape=(picture, picture, level),
        in_specs=[near, near, pl.BlockSpec(memory_space=pl.ANY)],
        out_specs=(near, near, far),
        scratch_shapes=[dma],
        compiler_params=pltpu.CompilerParams(vmem_limit_bytes=4 * 1024 * 1024),
        cost_estimate=pl.CostEstimate(flops=cells, bytes_accessed=8 * cells, transcendentals=0),
    )(*parts)
    return (first.transpose(0, 2, 1), second.transpose(0, 2, 1), field)


def solution(mesh):
    slabs, images = mesh.shape["depth"], mesh.shape["image"]

    def whole(level_set, velocity, view_flag, slab_rank):
        layers, rows, cols = level_set.shape
        dims = (slabs, images, layers // slabs, rows // images, cols)
        placed = (P("depth", "image", None), P(None, "depth", "image", None), P(), P())
        return jax.shard_map(
            functools.partial(local, dims),
            mesh=mesh,
            in_specs=placed,
            out_specs=(P(None, "image", "depth"), P(None, "image", "depth"), P("depth", "image", None)),
            check_vma=False,
        )(level_set, velocity, view_flag, slab_rank)

    return whole
```

```python
import functools

import jax
import jax.numpy as jnp
from jax import lax
from jax.experimental import pallas as pl
from jax.experimental.pallas import tpu as pltpu
from jax.sharding import PartitionSpec as P

STEPS = 4
DT = 0.3
CHUNKS = 2
MESH = pl.DeviceIdType.MESH


def kernel(dims, plan_hbm, field_hbm, speed_hbm, image_a, image_b, lev_4,
           lev_0, lev_1, lev_2, lev_3, plan_ref, vel, zh, xh, xsnd, pk, rc_a, rc_b, order, load_sem, zs, zr, xs, xr, ss, rs, own_sem):
    slabs, images, layers, rows, cols = dims
    tiles, pieces = rows // 8, cols // 128
    width = cols // slabs
    per = 128 // width
    scale = 2.0 / (layers * slabs)
    d = lax.axis_index("depth")
    i = lax.axis_index("image")
    d_up, d_dn = lax.rem(d + 1, slabs), lax.rem(d + slabs - 1, slabs)
    i_up, i_dn = lax.rem(i + 1, images), lax.rem(i + images - 1, images)

    rc = (rc_a, rc_b)
    fld = (lev_0, lev_1, lev_2, lev_3, lev_4)

    barrier = pltpu.get_barrier_semaphore()

    @pl.loop(1, slabs)
    def _(k):
        pl.semaphore_signal(barrier, inc=1, device_id={"depth": lax.rem(d + k, slabs)}, device_id_type=MESH)

    for other in (i_up, i_dn):
        pl.semaphore_signal(barrier, inc=1, device_id={"image": other}, device_id_type=MESH)

    load_field = pltpu.make_async_copy(field_hbm, fld[0], load_sem.at[0])
    load_speed = pltpu.make_async_copy(speed_hbm, vel, load_sem.at[1])
    load_plan = pltpu.make_async_copy(plan_hbm, plan_ref, load_sem.at[2])
    load_field.start()
    load_plan.start()
    load_speed.start()

    lane = lax.broadcasted_iota(jnp.int32, (8, 128), 1)
    sub = lax.broadcasted_iota(jnp.int32, (8, 128), 0)
    block = lane // width

    def z_copy(s, side):
        return pltpu.make_async_remote_copy(fld[s].at[0 if side else layers - 1], zh.at[side, s], zs.at[side, s], zr.at[side, s],
                                            device_id={"depth": d_dn if side else d_up}, device_id_type=MESH)

    inner = layers - 2

    def slot(z, kind):
        return {"first": inner, "last": inner + 1}.get(kind, z - 1)

    spans = ((0, inner // 2 + 1), (inner // 2 + 1, inner // 2 - 1), (inner, 2))

    def x_copy(s, part, side):
        where = pl.ds(*spans[part])
        return pltpu.make_async_remote_copy(xsnd.at[side, s, where], xh.at[side, s, where], xs.at[part, side, s], xr.at[part, side, s],
                                            device_id={"image": i_dn if side else i_up}, device_id_type=MESH)

    def start_z(s, side):
        @pl.when(d != (0 if side else slabs - 1))
        def _():
            z_copy(s, side).start()

    def wait_z(s, side):
        @pl.when(d != (slabs - 1 if side else 0))
        def _():
            z_copy(s, side).wait_recv()

    def start_x(s, part):
        for side in range(2):
            @pl.when(i != (0 if side else images - 1))
            def _():
                x_copy(s, part, side).start()

    def wait_x(s, part):
        for side in range(2):
            @pl.when(i != (images - 1 if side else 0))
            def _():
                x_copy(s, part, side).wait_recv()

    def empty_edges():
        for side in range(2):
            @pl.when(d == (slabs - 1 if side else 0))
            def _():
                zh[side] = jnp.zeros((STEPS, rows, cols), jnp.float32)

            @pl.when(i == (images - 1 if side else 0))
            def _():
                xh[side] = jnp.zeros((STEPS, layers, 1, cols), jnp.float32)

    def hop(n):
        return jnp.where(lax.rem(n, 2) == 0, n // 2 + 1, slabs - (n + 1) // 2)

    def send(f, ch, n):
        k = hop(n)
        to = lax.rem(d + k, slabs)
        pltpu.make_async_remote_copy(pk.at[f, to, ch], rc[f].at[d, ch], ss.at[f, ch, k], rs.at[f, ch, k],
                                     device_id={"depth": to}, device_id_type=MESH).start()

    def send_chunk(f, ch):
        pltpu.make_async_copy(pk.at[f, d, ch], rc[f].at[d, ch], own_sem.at[f, ch]).start()

        @pl.loop(0, slabs - 1)
        def _(n):
            send(f, ch, n)

    def send_half(f, ch, half):
        if half == 0:
            pltpu.make_async_copy(pk.at[f, d, ch], rc[f].at[d, ch], own_sem.at[f, ch]).start()

        @pl.loop(0, slabs // 2 - half)
        def _(m):
            send(f, ch, (m // 2) * 4 + lax.rem(m, 2) + 2 * half)

    def chunk_copy(f, ch, k):
        to, source = lax.rem(d + k, slabs), lax.rem(d + slabs - k, slabs)
        return pltpu.make_async_remote_copy(pk.at[f, to, ch], rc[f].at[source, ch], ss.at[f, ch, k], rs.at[f, ch, k],
                                            device_id={"depth": to}, device_id_type=MESH)

    def wait_chunk(f, ch):
        pltpu.make_async_copy(pk.at[f, d, ch], rc[f].at[d, ch], own_sem.at[f, ch]).wait()

        @pl.loop(1, slabs)
        def _(k):
            chunk_copy(f, ch, k).wait_recv()

    def tile_rows(t):
        if isinstance(t, int):
            return pl.ds(t * 8, 8)
        return pl.ds(pl.multiple_of(t * 8, 8), 8)

    def advance(s, z, t, z_lo, z_hi, x_lo, x_hi):
        here = tile_rows(t)
        centers = [fld[s][z, here, pl.ds(j * 128, 128)] for j in range(pieces)]
        right = [pltpu.roll(c, 1, 1) for c in centers]
        left = [pltpu.roll(c, 127, 1) for c in centers]
        zero = jnp.zeros((8, 128), jnp.float32)
        made = []
        for j in range(pieces):
            col = pl.ds(j * 128, 128)
            c = centers[j]
            y_lo = jnp.where(lane == 0, right[j - 1] if j > 0 else zero, right[j])
            y_hi = jnp.where(lane == 127, left[j + 1] if j < pieces - 1 else zero, left[j])
            low = z_lo(here, col)
            high = z_hi(here, col)
            if x_lo is None:
                x_low = pltpu.roll(jnp.where(sub == 7, fld[s][z, tile_rows(t - 1), col], c), 1, 0)
            else:
                x_low = jnp.where(sub == 0, x_lo(col), pltpu.roll(c, 1, 0))
            if x_hi is None:
                x_high = pltpu.roll(jnp.where(sub == 0, fld[s][z, tile_rows(t + 1), col], c), 7, 0)
            else:
                x_high = jnp.where(sub == 7, x_hi(col), pltpu.roll(c, 7, 0))
            rate = None
            for k, (lo, hi) in enumerate(((low, high), (x_low, x_high), (y_lo, y_hi))):
                u = vel[k, z, here, col]
                term = jnp.abs(u) * (c - jnp.where(u > 0.0, lo, hi))
                rate = term if rate is None else rate + term
            new = c - DT * rate
            fld[s + 1][z, here, col] = new
            made.append(new)
        return made

    def neighbours(s, z, kind):
        z_lo = (lambda r, c: zh[0, s, r, c]) if kind == "first" else (lambda r, c: fld[s][z - 1, r, c])
        z_hi = (lambda r, c: zh[1, s, r, c]) if kind == "last" else (lambda r, c: fld[s][z + 1, r, c])
        return z_lo, z_hi

    def keep_rows(s, place, made, side):
        for j in range(pieces):
            edge = made[j][7:8] if side == 0 else made[j][0:1]
            xsnd[side, s, place, :, pl.ds(j * 128, 128)] = edge

    def edge_tiles(s, z, kind):
        z_lo, z_hi = neighbours(s, z, kind)
        low = advance(s, z, 0, z_lo, z_hi, lambda c: xh[0, s, slot(z, kind), :, c], None)
        high = advance(s, z, tiles - 1, z_lo, z_hi, None, lambda c: xh[1, s, slot(z, kind), :, c])
        return low, high

    def layer(s, z, kind, keep):
        low, high = edge_tiles(s, z, kind)
        if keep:
            keep_rows(s + 1, slot(z, kind), low, 1)
            keep_rows(s + 1, slot(z, kind), high, 0)
        z_lo, z_hi = neighbours(s, z, kind)

        for t in range(1, tiles - 1):
            advance(s, z, t, z_lo, z_hi, None, None)

    def sides(s, part, keep):
        first, count = spans[part]

        @pl.loop(0, count // 2)
        def _(pair):
            for z in (first + 1 + 2 * pair, first + 2 + 2 * pair):
                low, high = edge_tiles(s, z, "inner")
                if keep:
                    keep_rows(s + 1, slot(z, "inner"), low, 1)
                    keep_rows(s + 1, slot(z, "inner"), high, 0)

    def interior(s):
        @pl.loop(1, layers - 1)
        def _(z):
            z_lo, z_hi = neighbours(s, z, "inner")

            for t in range(1, tiles - 1):
                advance(s, z, t, z_lo, z_hi, None, None)

    def turn(parts):
        turned = []
        for k in range(per):
            mixed = parts[k]
            for q in range(1, per):
                mixed = jnp.where(block == q, parts[(q + k) % per], mixed)
            turned.append(pltpu.roll(mixed, width * k, 1) if k else mixed)
        made = []
        for q in range(per):
            packed = turned[(-q) % per]
            for g in range(1, per):
                packed = jnp.where(block == g, turned[(g - q) % per], packed)
            made.append(packed)
        return made

    def render(s, f, ch):
        flag = plan_ref[d]
        one, zero = jnp.ones((8, 128), jnp.float32), jnp.zeros((8, 128), jnp.float32)

        @pl.loop(0, pieces)
        def _(j):
            col = pl.ds(pl.multiple_of(j * 128, 128), 128)

            def group(n0, carry):
                carry = [list(c) for c in carry]
                for q in range(4):
                    n = n0 * 4 + q
                    z = jnp.where(flag == 0, n, layers - 1 - n)
                    for g in range(per):
                        through, odd, green, total = carry[g]
                        x = fld[s][z, tile_rows(g * CHUNKS + ch), col]
                        bell = jnp.exp(-(x * x))
                        density = scale * bell
                        weight = through * (1.0 - jnp.exp(-density))
                        carry[g] = [through - weight, odd + weight * jnp.tanh(x), green + weight * bell, total + density]
                return tuple(tuple(c) for c in carry)

            carry = lax.fori_loop(0, layers // 4, group, tuple((one, zero, zero, zero) for _ in range(per)))
            for c in range(3):
                for q, packed in enumerate(turn([carry[g][c + 1] for g in range(per)])):
                    pk[f, per * j + q, ch, c] = packed

    def composite(f, ch, image):
        slots = [order[r] for r in range(slabs)]
        depth = odd = green = jnp.zeros((8, 128), jnp.float32)
        for r in range(slabs):
            through = jnp.exp(-depth)
            odd = odd + through * rc[f][slots[r], ch, 0]
            green = green + through * rc[f][slots[r], ch, 1]
            depth = depth + rc[f][slots[r], ch, 2]
        alpha = 1.0 - jnp.exp(-depth)
        for c, value in enumerate((0.5 * (alpha + odd), green, 0.5 * (alpha - odd), alpha)):
            image[c, pl.ds(8 * ch, 8), :] = value

    empty_edges()
    load_field.wait()
    load_plan.wait()

    def keep_first(z, kind):
        keep_rows(0, slot(z, kind), [fld[0][z, pl.ds(rows - 8, 8), pl.ds(j * 128, 128)] for j in range(pieces)], 0)
        keep_rows(0, slot(z, kind), [fld[0][z, pl.ds(0, 8), pl.ds(j * 128, 128)] for j in range(pieces)], 1)

    @pl.loop(1, layers - 1)
    def _(z):
        keep_first(z, "inner")

    keep_first(0, "first")
    keep_first(layers - 1, "last")
    for ch in range(CHUNKS):
        render(0, 0, ch)

    pl.semaphore_wait(barrier, slabs + 1)
    for part in range(3):
        start_x(0, part)
    for side in range(2):
        start_z(0, side)
    send_half(0, 0, 0)
    ranks = [plan_ref[slabs + b] for b in range(slabs)]
    for r in range(slabs):
        found = jnp.int32(0)
        for b in range(1, slabs):
            found = jnp.where(ranks[b] == r, b, found)
        order[r] = found
    load_speed.wait()
    interior(0)
    for s in range(STEPS - 1):
        for part in range(2):
            wait_x(s, part)
            sides(s, part, True)
            start_x(s + 1, part)
        wait_x(s, 2)
        wait_z(s, 0)
        layer(s, 0, "first", True)
        start_z(s + 1, 1)
        wait_z(s, 1)
        layer(s, layers - 1, "last", True)
        start_z(s + 1, 0)
        start_x(s + 1, 2)
        send_half(0, (s + 1) // 2, (s + 1) % 2)
        interior(s + 1)

    last = STEPS - 1
    for part in range(2):
        wait_x(last, part)
        sides(last, part, False)
    wait_x(last, 2)
    wait_z(last, 0)
    layer(last, 0, "first", False)
    wait_z(last, 1)
    layer(last, layers - 1, "last", False)
    for ch in range(CHUNKS):
        render(STEPS, 1, ch)
        send_chunk(1, ch)
    for f, image in ((0, image_a), (1, image_b)):
        for ch in range(CHUNKS):
            wait_chunk(f, ch)
        for ch in range(CHUNKS):
            composite(f, ch, image)

    for side in range(2):
        @pl.when(d != (0 if side else slabs - 1))
        def _():
            for s in range(STEPS):
                z_copy(s, side).wait_send()

        @pl.when(i != (0 if side else images - 1))
        def _():
            for s in range(STEPS):
                for part in range(3):
                    x_copy(s, part, side).wait_send()

    @pl.loop(0, CHUNKS)
    def _(ch):
        for f in range(2):
            @pl.loop(1, slabs)
            def _(k):
                chunk_copy(f, ch, k).wait_send()


def finish(image_a, image_b, field, first, second, next_hbm, picture, sem, out_sem):
    layers = field.shape[0]
    quarter = layers // 4
    copies = [pltpu.make_async_copy(field.at[pl.ds(q * quarter, quarter)], next_hbm.at[pl.ds(q * quarter, quarter)], sem.at[q]) for q in range(4)]
    for copy in copies:
        copy.start()
    for f, (image, out) in enumerate(((image_a, first), (image_b, second))):
        width = out.shape[1]
        for c in range(out.shape[0]):
            turned = image[c].T
            groups = turned.shape[0] // width
            picture[f, c] = jnp.concatenate([turned[g * width:(g + 1) * width] for g in range(groups)], axis=1)
        copies.append(pltpu.make_async_copy(picture.at[f], out, out_sem.at[f]))
        copies[-1].start()
    for copy in copies:
        copy.wait()


def local(dims, level_set, velocity, view_flag, slab_rank):
    slabs, images, layers, rows, cols = dims
    f32 = jnp.float32
    dma = pltpu.SemaphoreType.DMA
    cells = layers * rows * cols
    level = jax.ShapeDtypeStruct((layers, rows, cols), f32)
    packed = jax.ShapeDtypeStruct((4, 8 * CHUNKS, 128), f32)
    near = pl.BlockSpec(memory_space=pltpu.VMEM)
    far = pl.BlockSpec(memory_space=pltpu.HBM)
    parts = pl.pallas_call(
        functools.partial(kernel, dims),
        out_shape=(packed, packed, level),
        in_specs=[far] * 3,
        out_specs=(near, near, near),
        scratch_shapes=[pltpu.VMEM((layers, rows, cols), f32)] * 4 + [
            pltpu.SMEM((2 * slabs,), jnp.int32),
            pltpu.VMEM((3, layers, rows, cols), f32),
            pltpu.VMEM((2, STEPS, rows, cols), f32),
            pltpu.VMEM((2, STEPS, layers, 1, cols), f32),
            pltpu.VMEM((2, STEPS, layers, 1, cols), f32),
            pltpu.VMEM((2, slabs, CHUNKS, 3, 8, 128), f32),
            pltpu.VMEM((slabs, CHUNKS, 3, 8, 128), f32),
            pltpu.VMEM((slabs, CHUNKS, 3, 8, 128), f32),
            pltpu.SMEM((slabs,), jnp.int32),
            dma((3,)),
            dma((2, STEPS)),
            dma((2, STEPS)),
            dma((3, 2, STEPS)),
            dma((3, 2, STEPS)),
            dma((2, CHUNKS, slabs)),
            dma((2, CHUNKS, slabs)),
            dma((2, CHUNKS)),
        ],
        compiler_params=pltpu.CompilerParams(collective_id=0, has_side_effects=True, vmem_limit_bytes=51 * 1024 * 1024),
        cost_estimate=pl.CostEstimate(flops=1000000 * cells, bytes_accessed=0 * cells, transcendentals=6 * cells),
    )(jnp.concatenate([view_flag, slab_rank]), level_set, velocity)
    picture = jax.ShapeDtypeStruct((4, cols // slabs, rows), f32)
    first, second, field = pl.pallas_call(
        finish,
        out_shape=(picture, picture, level),
        in_specs=[near, near, pl.BlockSpec(memory_space=pl.ANY)],
        out_specs=(far, far, far),
        scratch_shapes=[pltpu.VMEM((2, 4, cols // slabs, rows), f32), dma((4,)), dma((2,))],
        compiler_params=pltpu.CompilerParams(vmem_limit_bytes=4 * 1024 * 1024),
        cost_estimate=pl.CostEstimate(flops=cells, bytes_accessed=8 * cells, transcendentals=0),
    )(*parts)
    return (first.transpose(0, 2, 1), second.transpose(0, 2, 1), field)


def solution(mesh):
    slabs, images = mesh.shape["depth"], mesh.shape["image"]

    def whole(level_set, velocity, view_flag, slab_rank):
        layers, rows, cols = level_set.shape
        dims = (slabs, images, layers // slabs, rows // images, cols)
        placed = (P("depth", "image", None), P(None, "depth", "image", None), P(), P())
        return jax.shard_map(
            functools.partial(local, dims),
            mesh=mesh,
            in_specs=placed,
            out_specs=(P(None, "image", "depth"), P(None, "image", "depth"), P("depth", "image", None)),
            check_vma=False,
        )(level_set, velocity, view_flag, slab_rank)

    return whole
```

```python
import functools

import jax
import jax.numpy as jnp
from jax import lax
from jax.experimental import pallas as pl
from jax.experimental.pallas import tpu as pltpu
from jax.sharding import PartitionSpec as P

STEPS = 4
DT = 0.3
CHUNKS = 2
MESH = pl.DeviceIdType.MESH


def kernel(dims, plan_hbm, field_hbm, speed_hbm, image_a, image_b, lev_4,
           lev_0, lev_1, lev_2, lev_3, plan_ref, vel, zh, xh, xsnd, pk, rc_a, rc_b, order, load_sem, zs, zr, xs, xr, ss, rs, own_sem):
    slabs, images, layers, rows, cols = dims
    tiles, pieces = rows // 8, cols // 128
    width = cols // slabs
    per = 128 // width
    scale = 2.0 / (layers * slabs)
    d = lax.axis_index("depth")
    i = lax.axis_index("image")
    d_up, d_dn = lax.rem(d + 1, slabs), lax.rem(d + slabs - 1, slabs)
    i_up, i_dn = lax.rem(i + 1, images), lax.rem(i + images - 1, images)

    rc = (rc_a, rc_b)
    fld = (lev_0, lev_1, lev_2, lev_3, lev_4)

    barrier = pltpu.get_barrier_semaphore()

    @pl.loop(1, slabs)
    def _(k):
        pl.semaphore_signal(barrier, inc=1, device_id={"depth": lax.rem(d + k, slabs)}, device_id_type=MESH)

    for other in (i_up, i_dn):
        pl.semaphore_signal(barrier, inc=1, device_id={"image": other}, device_id_type=MESH)

    load_field = pltpu.make_async_copy(field_hbm, fld[0], load_sem.at[0])
    load_speed = pltpu.make_async_copy(speed_hbm, vel, load_sem.at[1])
    load_plan = pltpu.make_async_copy(plan_hbm, plan_ref, load_sem.at[2])
    load_field.start()
    load_plan.start()
    load_speed.start()

    lane = lax.broadcasted_iota(jnp.int32, (8, 128), 1)
    sub = lax.broadcasted_iota(jnp.int32, (8, 128), 0)
    block = lane // width

    def z_copy(s, side):
        return pltpu.make_async_remote_copy(fld[s].at[0 if side else layers - 1], zh.at[side, s], zs.at[side, s], zr.at[side, s],
                                            device_id={"depth": d_dn if side else d_up}, device_id_type=MESH)

    inner = layers - 2

    def slot(z, kind):
        return {"first": inner, "last": inner + 1}.get(kind, z - 1)

    spans = ((0, inner // 2 + 1), (inner // 2 + 1, inner // 2 - 1), (inner, 2))

    def x_copy(s, part, side):
        where = pl.ds(*spans[part])
        return pltpu.make_async_remote_copy(xsnd.at[side, s, where], xh.at[side, s, where], xs.at[part, side, s], xr.at[part, side, s],
                                            device_id={"image": i_dn if side else i_up}, device_id_type=MESH)

    def start_z(s, side):
        @pl.when(d != (0 if side else slabs - 1))
        def _():
            z_copy(s, side).start()

    def wait_z(s, side):
        @pl.when(d != (slabs - 1 if side else 0))
        def _():
            z_copy(s, side).wait_recv()

    def start_x(s, part):
        for side in range(2):
            @pl.when(i != (0 if side else images - 1))
            def _():
                x_copy(s, part, side).start()

    def wait_x(s, part):
        for side in range(2):
            @pl.when(i != (images - 1 if side else 0))
            def _():
                x_copy(s, part, side).wait_recv()

    def empty_edges():
        for side in range(2):
            @pl.when(d == (slabs - 1 if side else 0))
            def _():
                zh[side] = jnp.zeros((STEPS, rows, cols), jnp.float32)

            @pl.when(i == (images - 1 if side else 0))
            def _():
                xh[side] = jnp.zeros((STEPS, layers, 1, cols), jnp.float32)

    def hop(n):
        return jnp.where(lax.rem(n, 2) == 0, n // 2 + 1, slabs - (n + 1) // 2)

    def send(f, ch, n):
        k = hop(slabs - 2 - n)
        to = lax.rem(d + k, slabs)
        pltpu.make_async_remote_copy(pk.at[f, to, ch], rc[f].at[d, ch], ss.at[f, ch, k], rs.at[f, ch, k],
                                     device_id={"depth": to}, device_id_type=MESH).start()

    def send_chunk(f, ch):
        pltpu.make_async_copy(pk.at[f, d, ch], rc[f].at[d, ch], own_sem.at[f, ch]).start()

        @pl.loop(0, slabs - 1)
        def _(n):
            send(f, ch, n)

    def send_half(f, ch, half):
        if half == 0:
            pltpu.make_async_copy(pk.at[f, d, ch], rc[f].at[d, ch], own_sem.at[f, ch]).start()

        @pl.loop(0, slabs // 2 - half)
        def _(m):
            send(f, ch, (m // 2) * 4 + lax.rem(m, 2) + 2 * half)

    def chunk_copy(f, ch, k):
        to, source = lax.rem(d + k, slabs), lax.rem(d + slabs - k, slabs)
        return pltpu.make_async_remote_copy(pk.at[f, to, ch], rc[f].at[source, ch], ss.at[f, ch, k], rs.at[f, ch, k],
                                            device_id={"depth": to}, device_id_type=MESH)

    def wait_chunk(f, ch):
        pltpu.make_async_copy(pk.at[f, d, ch], rc[f].at[d, ch], own_sem.at[f, ch]).wait()

        @pl.loop(1, slabs)
        def _(k):
            chunk_copy(f, ch, k).wait_recv()

    def tile_rows(t):
        if isinstance(t, int):
            return pl.ds(t * 8, 8)
        return pl.ds(pl.multiple_of(t * 8, 8), 8)

    def advance(s, z, t, z_lo, z_hi, x_lo, x_hi):
        here = tile_rows(t)
        centers = [fld[s][z, here, pl.ds(j * 128, 128)] for j in range(pieces)]
        right = [pltpu.roll(c, 1, 1) for c in centers]
        left = [pltpu.roll(c, 127, 1) for c in centers]
        zero = jnp.zeros((8, 128), jnp.float32)
        made = []
        for j in range(pieces):
            col = pl.ds(j * 128, 128)
            c = centers[j]
            y_lo = jnp.where(lane == 0, right[j - 1] if j > 0 else zero, right[j])
            y_hi = jnp.where(lane == 127, left[j + 1] if j < pieces - 1 else zero, left[j])
            low = z_lo(here, col)
            high = z_hi(here, col)
            if x_lo is None:
                x_low = pltpu.roll(jnp.where(sub == 7, fld[s][z, tile_rows(t - 1), col], c), 1, 0)
            else:
                x_low = jnp.where(sub == 0, x_lo(col), pltpu.roll(c, 1, 0))
            if x_hi is None:
                x_high = pltpu.roll(jnp.where(sub == 0, fld[s][z, tile_rows(t + 1), col], c), 7, 0)
            else:
                x_high = jnp.where(sub == 7, x_hi(col), pltpu.roll(c, 7, 0))
            rate = None
            for k, (lo, hi) in enumerate(((low, high), (x_low, x_high), (y_lo, y_hi))):
                u = vel[k, z, here, col]
                term = jnp.abs(u) * (c - jnp.where(u > 0.0, lo, hi))
                rate = term if rate is None else rate + term
            new = c - DT * rate
            fld[s + 1][z, here, col] = new
            made.append(new)
        return made

    def neighbours(s, z, kind):
        z_lo = (lambda r, c: zh[0, s, r, c]) if kind == "first" else (lambda r, c: fld[s][z - 1, r, c])
        z_hi = (lambda r, c: zh[1, s, r, c]) if kind == "last" else (lambda r, c: fld[s][z + 1, r, c])
        return z_lo, z_hi

    def keep_rows(s, place, made, side):
        for j in range(pieces):
            edge = made[j][7:8] if side == 0 else made[j][0:1]
            xsnd[side, s, place, :, pl.ds(j * 128, 128)] = edge

    def edge_tiles(s, z, kind):
        z_lo, z_hi = neighbours(s, z, kind)
        low = advance(s, z, 0, z_lo, z_hi, lambda c: xh[0, s, slot(z, kind), :, c], None)
        high = advance(s, z, tiles - 1, z_lo, z_hi, None, lambda c: xh[1, s, slot(z, kind), :, c])
        return low, high

    def layer(s, z, kind, keep):
        low, high = edge_tiles(s, z, kind)
        if keep:
            keep_rows(s + 1, slot(z, kind), low, 1)
            keep_rows(s + 1, slot(z, kind), high, 0)
        z_lo, z_hi = neighbours(s, z, kind)

        for t in range(1, tiles - 1):
            advance(s, z, t, z_lo, z_hi, None, None)

    def sides(s, part, keep):
        first, count = spans[part]

        @pl.loop(0, count // 2)
        def _(pair):
            for z in (first + 1 + 2 * pair, first + 2 + 2 * pair):
                low, high = edge_tiles(s, z, "inner")
                if keep:
                    keep_rows(s + 1, slot(z, "inner"), low, 1)
                    keep_rows(s + 1, slot(z, "inner"), high, 0)

    def edges(s, z, kind, t):
        x_lo = (lambda c: xh[0, s, slot(z, kind), :, c]) if t == 0 else None
        x_hi = (lambda c: xh[1, s, slot(z, kind), :, c]) if t == tiles - 1 else None
        z_lo, z_hi = neighbours(s, z, kind)
        advance(s, z, t, z_lo, z_hi, x_lo, x_hi)

    def last_rows(s, ch):
        @pl.loop(0, 2)
        def _(half):
            for q in range(inner // 2):
                edges(s, 1 + half * (inner // 2) + q, "inner", ch * (tiles - 1))

        for z, kind in ((0, "first"), (layers - 1, "last")):
            for t in range(ch, tiles, CHUNKS):
                edges(s, z, kind, t)

    def interior(s):
        @pl.loop(1, layers - 1)
        def _(z):
            z_lo, z_hi = neighbours(s, z, "inner")

            for t in range(1, tiles - 1):
                advance(s, z, t, z_lo, z_hi, None, None)

    def turn(parts):
        turned = []
        for k in range(per):
            mixed = parts[k]
            for q in range(1, per):
                mixed = jnp.where(block == q, parts[(q + k) % per], mixed)
            turned.append(pltpu.roll(mixed, width * k, 1) if k else mixed)
        made = []
        for q in range(per):
            packed = turned[(-q) % per]
            for g in range(1, per):
                packed = jnp.where(block == g, turned[(g - q) % per], packed)
            made.append(packed)
        return made

    def render(s, f, ch):
        flag = plan_ref[d]
        one, zero = jnp.ones((8, 128), jnp.float32), jnp.zeros((8, 128), jnp.float32)

        @pl.loop(0, pieces)
        def _(j):
            col = pl.ds(pl.multiple_of(j * 128, 128), 128)

            def group(n0, carry):
                carry = [list(c) for c in carry]
                for q in range(4):
                    n = n0 * 4 + q
                    z = jnp.where(flag == 0, n, layers - 1 - n)
                    for g in range(per):
                        through, odd, green, total = carry[g]
                        x = fld[s][z, tile_rows(g * CHUNKS + ch), col]
                        bell = jnp.exp(-(x * x))
                        density = scale * bell
                        weight = through * (1.0 - jnp.exp(-density))
                        carry[g] = [through - weight, odd + weight * jnp.tanh(x), green + weight * bell, total + density]
                return tuple(tuple(c) for c in carry)

            carry = lax.fori_loop(0, layers // 4, group, tuple((one, zero, zero, zero) for _ in range(per)))
            for c in range(3):
                for q, packed in enumerate(turn([carry[g][c + 1] for g in range(per)])):
                    pk[f, per * j + q, ch, c] = packed

    def composite(f, ch, image):
        slots = [order[r] for r in range(slabs)]
        depth = odd = green = jnp.zeros((8, 128), jnp.float32)
        for r in range(slabs):
            through = jnp.exp(-depth)
            odd = odd + through * rc[f][slots[r], ch, 0]
            green = green + through * rc[f][slots[r], ch, 1]
            depth = depth + rc[f][slots[r], ch, 2]
        alpha = 1.0 - jnp.exp(-depth)
        for c, value in enumerate((0.5 * (alpha + odd), green, 0.5 * (alpha - odd), alpha)):
            image[c, pl.ds(8 * ch, 8), :] = value

    empty_edges()
    load_field.wait()
    load_plan.wait()

    def keep_first(z, kind):
        keep_rows(0, slot(z, kind), [fld[0][z, pl.ds(rows - 8, 8), pl.ds(j * 128, 128)] for j in range(pieces)], 0)
        keep_rows(0, slot(z, kind), [fld[0][z, pl.ds(0, 8), pl.ds(j * 128, 128)] for j in range(pieces)], 1)

    @pl.loop(1, layers - 1)
    def _(z):
        keep_first(z, "inner")

    keep_first(0, "first")
    keep_first(layers - 1, "last")
    render(0, 0, 0)

    pl.semaphore_wait(barrier, slabs + 1)
    for part in range(3):
        start_x(0, part)
    for side in range(2):
        start_z(0, side)
    send_half(0, 0, 0)
    ranks = [plan_ref[slabs + b] for b in range(slabs)]
    for r in range(slabs):
        found = jnp.int32(0)
        for b in range(1, slabs):
            found = jnp.where(ranks[b] == r, b, found)
        order[r] = found
    load_speed.wait()
    interior(0)
    for ch in range(1, CHUNKS):
        render(0, 0, ch)
    for s in range(STEPS - 1):
        for part in range(2):
            wait_x(s, part)
            sides(s, part, True)
            start_x(s + 1, part)
        wait_x(s, 2)
        wait_z(s, 0)
        layer(s, 0, "first", True)
        start_z(s + 1, 1)
        wait_z(s, 1)
        layer(s, layers - 1, "last", True)
        start_z(s + 1, 0)
        start_x(s + 1, 2)
        send_half(0, (s + 1) // 2, (s + 1) % 2)
        interior(s + 1)

    last = STEPS - 1
    for part in range(3):
        wait_x(last, part)
    for side in range(2):
        wait_z(last, side)
    for ch in range(CHUNKS):
        last_rows(last, ch)
        render(STEPS, 1, ch)
        send_chunk(1, ch)

    def wait_sends(f):
        for ch in range(CHUNKS):
            @pl.loop(1, slabs)
            def _(k):
                chunk_copy(f, ch, k).wait_send()

    for ch in range(CHUNKS):
        wait_chunk(0, ch)
    for ch in range(CHUNKS):
        composite(0, ch, image_a)

    for side in range(2):
        @pl.when(d != (0 if side else slabs - 1))
        def _():
            for s in range(STEPS):
                z_copy(s, side).wait_send()

        @pl.when(i != (0 if side else images - 1))
        def _():
            for s in range(STEPS):
                for part in range(3):
                    x_copy(s, part, side).wait_send()

    wait_sends(0)
    wait_sends(1)
    for ch in range(CHUNKS):
        wait_chunk(1, ch)
    for ch in range(CHUNKS):
        composite(1, ch, image_b)


def finish(image_a, image_b, field, first, second, next_hbm, picture, sem, out_sem):
    layers = field.shape[0]
    quarter = layers // 4
    copies = [pltpu.make_async_copy(field.at[pl.ds(q * quarter, quarter)], next_hbm.at[pl.ds(q * quarter, quarter)], sem.at[q]) for q in range(4)]
    for copy in copies:
        copy.start()
    for f, (image, out) in enumerate(((image_a, first), (image_b, second))):
        width = out.shape[1]
        for c in range(out.shape[0]):
            turned = image[c].T
            groups = turned.shape[0] // width
            picture[f, c] = jnp.concatenate([turned[g * width:(g + 1) * width] for g in range(groups)], axis=1)
        copies.append(pltpu.make_async_copy(picture.at[f], out, out_sem.at[f]))
        copies[-1].start()
    for copy in copies:
        copy.wait()


def local(dims, level_set, velocity, view_flag, slab_rank):
    slabs, images, layers, rows, cols = dims
    f32 = jnp.float32
    dma = pltpu.SemaphoreType.DMA
    cells = layers * rows * cols
    level = jax.ShapeDtypeStruct((layers, rows, cols), f32)
    packed = jax.ShapeDtypeStruct((4, 8 * CHUNKS, 128), f32)
    near = pl.BlockSpec(memory_space=pltpu.VMEM)
    far = pl.BlockSpec(memory_space=pltpu.HBM)
    parts = pl.pallas_call(
        functools.partial(kernel, dims),
        out_shape=(packed, packed, level),
        in_specs=[far] * 3,
        out_specs=(near, near, near),
        scratch_shapes=[pltpu.VMEM((layers, rows, cols), f32)] * 4 + [
            pltpu.SMEM((2 * slabs,), jnp.int32),
            pltpu.VMEM((3, layers, rows, cols), f32),
            pltpu.VMEM((2, STEPS, rows, cols), f32),
            pltpu.VMEM((2, STEPS, layers, 1, cols), f32),
            pltpu.VMEM((2, STEPS, layers, 1, cols), f32),
            pltpu.VMEM((2, slabs, CHUNKS, 3, 8, 128), f32),
            pltpu.VMEM((slabs, CHUNKS, 3, 8, 128), f32),
            pltpu.VMEM((slabs, CHUNKS, 3, 8, 128), f32),
            pltpu.SMEM((slabs,), jnp.int32),
            dma((3,)),
            dma((2, STEPS)),
            dma((2, STEPS)),
            dma((3, 2, STEPS)),
            dma((3, 2, STEPS)),
            dma((2, CHUNKS, slabs)),
            dma((2, CHUNKS, slabs)),
            dma((2, CHUNKS)),
        ],
        compiler_params=pltpu.CompilerParams(collective_id=0, has_side_effects=True, vmem_limit_bytes=51 * 1024 * 1024),
        cost_estimate=pl.CostEstimate(flops=1000000 * cells, bytes_accessed=0 * cells, transcendentals=6 * cells),
    )(jnp.concatenate([view_flag, slab_rank]), level_set, velocity)
    picture = jax.ShapeDtypeStruct((4, cols // slabs, rows), f32)
    first, second, field = pl.pallas_call(
        finish,
        out_shape=(picture, picture, level),
        in_specs=[near, near, pl.BlockSpec(memory_space=pl.ANY)],
        out_specs=(far, far, far),
        scratch_shapes=[pltpu.VMEM((2, 4, cols // slabs, rows), f32), dma((4,)), dma((2,))],
        compiler_params=pltpu.CompilerParams(vmem_limit_bytes=4 * 1024 * 1024),
        cost_estimate=pl.CostEstimate(flops=cells, bytes_accessed=8 * cells, transcendentals=0),
    )(*parts)
    return (first.transpose(0, 2, 1), second.transpose(0, 2, 1), field)


def solution(mesh):
    slabs, images = mesh.shape["depth"], mesh.shape["image"]

    def whole(level_set, velocity, view_flag, slab_rank):
        layers, rows, cols = level_set.shape
        dims = (slabs, images, layers // slabs, rows // images, cols)
        placed = (P("depth", "image", None), P(None, "depth", "image", None), P(), P())
        return jax.shard_map(
            functools.partial(local, dims),
            mesh=mesh,
            in_specs=placed,
            out_specs=(P(None, "image", "depth"), P(None, "image", "depth"), P("depth", "image", None)),
            check_vma=False,
        )(level_set, velocity, view_flag, slab_rank)

    return whole
```

```python
import functools

import jax
import jax.numpy as jnp
from jax import lax
from jax.experimental import pallas as pl
from jax.experimental.pallas import tpu as pltpu
from jax.sharding import PartitionSpec as P

STEPS = 4
DT = 0.3
CHUNKS = 2
MESH = pl.DeviceIdType.MESH


def kernel(dims, plan_hbm, field_hbm, speed_hbm, image_a, image_b, lev_4,
           lev_0, lev_1, lev_2, lev_3, plan_ref, vel, zh, xh, xsnd, pk, rc_a, rc_b, order, load_sem, zs, zr, xs, xr, ss, rs, own_sem):
    slabs, images, layers, rows, cols = dims
    tiles, pieces = rows // 8, cols // 128
    width = cols // slabs
    per = 128 // width
    scale = 2.0 / (layers * slabs)
    d = lax.axis_index("depth")
    i = lax.axis_index("image")
    d_up, d_dn = lax.rem(d + 1, slabs), lax.rem(d + slabs - 1, slabs)
    i_up, i_dn = lax.rem(i + 1, images), lax.rem(i + images - 1, images)

    rc = (rc_a, rc_b)
    fld = (lev_0, lev_1, lev_2, lev_3, lev_4)

    barrier = pltpu.get_barrier_semaphore()

    @pl.loop(1, slabs)
    def _(k):
        pl.semaphore_signal(barrier, inc=1, device_id={"depth": lax.rem(d + k, slabs)}, device_id_type=MESH)

    for other in (i_up, i_dn):
        pl.semaphore_signal(barrier, inc=1, device_id={"image": other}, device_id_type=MESH)

    load_field = pltpu.make_async_copy(field_hbm, fld[0], load_sem.at[0])
    load_speed = pltpu.make_async_copy(speed_hbm, vel, load_sem.at[1])
    load_plan = pltpu.make_async_copy(plan_hbm, plan_ref, load_sem.at[2])
    load_field.start()
    load_plan.start()
    load_speed.start()

    lane = lax.broadcasted_iota(jnp.int32, (8, 128), 1)
    sub = lax.broadcasted_iota(jnp.int32, (8, 128), 0)
    block = lane // width

    def z_copy(s, side):
        return pltpu.make_async_remote_copy(fld[s].at[0 if side else layers - 1], zh.at[side, s], zs.at[side, s], zr.at[side, s],
                                            device_id={"depth": d_dn if side else d_up}, device_id_type=MESH)

    inner = layers - 2

    def slot(z, kind):
        return {"first": inner, "last": inner + 1}.get(kind, z - 1)

    spans = ((0, inner), (inner, 2))

    def x_copy(s, part, side):
        where = pl.ds(*spans[part])
        return pltpu.make_async_remote_copy(xsnd.at[side, s, where], xh.at[side, s, where], xs.at[part, side, s], xr.at[part, side, s],
                                            device_id={"image": i_dn if side else i_up}, device_id_type=MESH)

    def start_z(s, side):
        @pl.when(d != (0 if side else slabs - 1))
        def _():
            z_copy(s, side).start()

    def wait_z(s, side):
        @pl.when(d != (slabs - 1 if side else 0))
        def _():
            z_copy(s, side).wait_recv()

    def start_x(s, part):
        for side in range(2):
            @pl.when(i != (0 if side else images - 1))
            def _():
                x_copy(s, part, side).start()

    def wait_x(s, part):
        for side in range(2):
            @pl.when(i != (images - 1 if side else 0))
            def _():
                x_copy(s, part, side).wait_recv()

    def empty_edges():
        for side in range(2):
            @pl.when(d == (slabs - 1 if side else 0))
            def _():
                zh[side] = jnp.zeros((STEPS, rows, cols), jnp.float32)

            @pl.when(i == (images - 1 if side else 0))
            def _():
                xh[side] = jnp.zeros((STEPS, layers, 1, cols), jnp.float32)

    def hop(n):
        return jnp.where(lax.rem(n, 2) == 0, n // 2 + 1, slabs - (n + 1) // 2)

    def send(f, ch, n):
        k = hop(slabs - 2 - n)
        to = lax.rem(d + k, slabs)
        pltpu.make_async_remote_copy(pk.at[f, to, ch], rc[f].at[d, ch], ss.at[f, ch, k], rs.at[f, ch, k],
                                     device_id={"depth": to}, device_id_type=MESH).start()

    def send_chunk(f, ch):
        pltpu.make_async_copy(pk.at[f, d, ch], rc[f].at[d, ch], own_sem.at[f, ch]).start()

        @pl.loop(0, slabs - 1)
        def _(n):
            send(f, ch, n)

    def send_half(f, ch, half):
        if half == 0:
            pltpu.make_async_copy(pk.at[f, d, ch], rc[f].at[d, ch], own_sem.at[f, ch]).start()

        @pl.loop(0, slabs // 2 - half)
        def _(m):
            send(f, ch, (m // 2) * 4 + lax.rem(m, 2) + 2 * half)

    def chunk_copy(f, ch, k):
        to, source = lax.rem(d + k, slabs), lax.rem(d + slabs - k, slabs)
        return pltpu.make_async_remote_copy(pk.at[f, to, ch], rc[f].at[source, ch], ss.at[f, ch, k], rs.at[f, ch, k],
                                            device_id={"depth": to}, device_id_type=MESH)

    def wait_chunk(f, ch):
        pltpu.make_async_copy(pk.at[f, d, ch], rc[f].at[d, ch], own_sem.at[f, ch]).wait()

        @pl.loop(1, slabs)
        def _(k):
            chunk_copy(f, ch, k).wait_recv()

    def tile_rows(t):
        if isinstance(t, int):
            return pl.ds(t * 8, 8)
        return pl.ds(pl.multiple_of(t * 8, 8), 8)

    def advance(s, z, t, z_lo, z_hi, x_lo, x_hi):
        here = tile_rows(t)
        centers = [fld[s][z, here, pl.ds(j * 128, 128)] for j in range(pieces)]
        right = [pltpu.roll(c, 1, 1) for c in centers]
        left = [pltpu.roll(c, 127, 1) for c in centers]
        zero = jnp.zeros((8, 128), jnp.float32)
        made = []
        for j in range(pieces):
            col = pl.ds(j * 128, 128)
            c = centers[j]
            y_lo = jnp.where(lane == 0, right[j - 1] if j > 0 else zero, right[j])
            y_hi = jnp.where(lane == 127, left[j + 1] if j < pieces - 1 else zero, left[j])
            low = z_lo(here, col)
            high = z_hi(here, col)
            if x_lo is None:
                x_low = pltpu.roll(jnp.where(sub == 7, fld[s][z, tile_rows(t - 1), col], c), 1, 0)
            else:
                x_low = jnp.where(sub == 0, x_lo(col), pltpu.roll(c, 1, 0))
            if x_hi is None:
                x_high = pltpu.roll(jnp.where(sub == 0, fld[s][z, tile_rows(t + 1), col], c), 7, 0)
            else:
                x_high = jnp.where(sub == 7, x_hi(col), pltpu.roll(c, 7, 0))
            rate = None
            for k, (lo, hi) in enumerate(((low, high), (x_low, x_high), (y_lo, y_hi))):
                u = vel[k, z, here, col]
                term = jnp.abs(u) * (c - jnp.where(u > 0.0, lo, hi))
                rate = term if rate is None else rate + term
            new = c - DT * rate
            fld[s + 1][z, here, col] = new
            made.append(new)
        return made

    def neighbours(s, z, kind):
        z_lo = (lambda r, c: zh[0, s, r, c]) if kind == "first" else (lambda r, c: fld[s][z - 1, r, c])
        z_hi = (lambda r, c: zh[1, s, r, c]) if kind == "last" else (lambda r, c: fld[s][z + 1, r, c])
        return z_lo, z_hi

    def keep_rows(s, place, made, side):
        for j in range(pieces):
            edge = made[j][7:8] if side == 0 else made[j][0:1]
            xsnd[side, s, place, :, pl.ds(j * 128, 128)] = edge

    def edge_tiles(s, z, kind):
        z_lo, z_hi = neighbours(s, z, kind)
        low = advance(s, z, 0, z_lo, z_hi, lambda c: xh[0, s, slot(z, kind), :, c], None)
        high = advance(s, z, tiles - 1, z_lo, z_hi, None, lambda c: xh[1, s, slot(z, kind), :, c])
        return low, high

    def layer(s, z, kind, keep):
        low, high = edge_tiles(s, z, kind)
        if keep:
            keep_rows(s + 1, slot(z, kind), low, 1)
            keep_rows(s + 1, slot(z, kind), high, 0)
        z_lo, z_hi = neighbours(s, z, kind)

        for t in range(1, tiles - 1):
            advance(s, z, t, z_lo, z_hi, None, None)

    def sides(s, part, keep):
        first, count = spans[part]

        @pl.loop(0, count // 2)
        def _(pair):
            for z in (first + 1 + 2 * pair, first + 2 + 2 * pair):
                low, high = edge_tiles(s, z, "inner")
                if keep:
                    keep_rows(s + 1, slot(z, "inner"), low, 1)
                    keep_rows(s + 1, slot(z, "inner"), high, 0)

    def edges(s, z, kind, t):
        x_lo = (lambda c: xh[0, s, slot(z, kind), :, c]) if t == 0 else None
        x_hi = (lambda c: xh[1, s, slot(z, kind), :, c]) if t == tiles - 1 else None
        z_lo, z_hi = neighbours(s, z, kind)
        advance(s, z, t, z_lo, z_hi, x_lo, x_hi)

    def last_rows(s, ch):
        @pl.loop(0, 2)
        def _(half):
            for q in range(inner // 2):
                edges(s, 1 + half * (inner // 2) + q, "inner", ch * (tiles - 1))

        for z, kind in ((0, "first"), (layers - 1, "last")):
            for t in range(ch, tiles, CHUNKS):
                edges(s, z, kind, t)

    def interior(s):
        @pl.loop(1, layers - 1)
        def _(z):
            z_lo, z_hi = neighbours(s, z, "inner")

            for t in range(1, tiles - 1):
                advance(s, z, t, z_lo, z_hi, None, None)

    def turn(parts):
        turned = []
        for k in range(per):
            mixed = parts[k]
            for q in range(1, per):
                mixed = jnp.where(block == q, parts[(q + k) % per], mixed)
            turned.append(pltpu.roll(mixed, width * k, 1) if k else mixed)
        made = []
        for q in range(per):
            packed = turned[(-q) % per]
            for g in range(1, per):
                packed = jnp.where(block == g, turned[(g - q) % per], packed)
            made.append(packed)
        return made

    def render(s, f, ch):
        flag = plan_ref[d]
        one, zero = jnp.ones((8, 128), jnp.float32), jnp.zeros((8, 128), jnp.float32)

        @pl.loop(0, pieces)
        def _(j):
            col = pl.ds(pl.multiple_of(j * 128, 128), 128)

            def group(n0, carry):
                carry = [list(c) for c in carry]
                for q in range(4):
                    n = n0 * 4 + q
                    z = jnp.where(flag == 0, n, layers - 1 - n)
                    for g in range(per):
                        through, odd, green, total = carry[g]
                        x = fld[s][z, tile_rows(g * CHUNKS + ch), col]
                        bell = jnp.exp(-(x * x))
                        density = scale * bell
                        weight = through * (1.0 - jnp.exp(-density))
                        carry[g] = [through - weight, odd + weight * jnp.tanh(x), green + weight * bell, total + density]
                return tuple(tuple(c) for c in carry)

            carry = lax.fori_loop(0, layers // 4, group, tuple((one, zero, zero, zero) for _ in range(per)))
            for c in range(3):
                for q, packed in enumerate(turn([carry[g][c + 1] for g in range(per)])):
                    pk[f, per * j + q, ch, c] = packed

    def composite(f, ch, image):
        slots = [order[r] for r in range(slabs)]
        depth = odd = green = jnp.zeros((8, 128), jnp.float32)
        for r in range(slabs):
            through = jnp.exp(-depth)
            odd = odd + through * rc[f][slots[r], ch, 0]
            green = green + through * rc[f][slots[r], ch, 1]
            depth = depth + rc[f][slots[r], ch, 2]
        alpha = 1.0 - jnp.exp(-depth)
        for c, value in enumerate((0.5 * (alpha + odd), green, 0.5 * (alpha - odd), alpha)):
            image[c, pl.ds(8 * ch, 8), :] = value

    empty_edges()
    load_field.wait()
    load_plan.wait()

    def keep_first(z, kind):
        keep_rows(0, slot(z, kind), [fld[0][z, pl.ds(rows - 8, 8), pl.ds(j * 128, 128)] for j in range(pieces)], 0)
        keep_rows(0, slot(z, kind), [fld[0][z, pl.ds(0, 8), pl.ds(j * 128, 128)] for j in range(pieces)], 1)

    @pl.loop(1, layers - 1)
    def _(z):
        keep_first(z, "inner")

    keep_first(0, "first")
    keep_first(layers - 1, "last")
    render(0, 0, 0)

    pl.semaphore_wait(barrier, slabs + 1)
    for part in range(2):
        start_x(0, part)
    for side in range(2):
        start_z(0, side)
    send_half(0, 0, 0)
    ranks = [plan_ref[slabs + b] for b in range(slabs)]
    for r in range(slabs):
        found = jnp.int32(0)
        for b in range(1, slabs):
            found = jnp.where(ranks[b] == r, b, found)
        order[r] = found
    load_speed.wait()
    interior(0)
    for ch in range(1, CHUNKS):
        render(0, 0, ch)
    for s in range(STEPS - 1):
        wait_x(s, 0)
        sides(s, 0, True)
        start_x(s + 1, 0)
        wait_x(s, 1)
        wait_z(s, 0)
        layer(s, 0, "first", True)
        start_z(s + 1, 1)
        wait_z(s, 1)
        layer(s, layers - 1, "last", True)
        start_z(s + 1, 0)
        start_x(s + 1, 1)
        send_half(0, (s + 1) // 2, (s + 1) % 2)
        interior(s + 1)

    last = STEPS - 1
    for part in range(2):
        wait_x(last, part)
    for side in range(2):
        wait_z(last, side)
    for ch in range(CHUNKS):
        last_rows(last, ch)
        render(STEPS, 1, ch)
        send_chunk(1, ch)

    def wait_sends(f):
        for ch in range(CHUNKS):
            @pl.loop(1, slabs)
            def _(k):
                chunk_copy(f, ch, k).wait_send()

    for ch in range(CHUNKS):
        wait_chunk(0, ch)
    for ch in range(CHUNKS):
        composite(0, ch, image_a)

    for side in range(2):
        @pl.when(d != (0 if side else slabs - 1))
        def _():
            for s in range(STEPS):
                z_copy(s, side).wait_send()

        @pl.when(i != (0 if side else images - 1))
        def _():
            for s in range(STEPS):
                for part in range(2):
                    x_copy(s, part, side).wait_send()

    wait_sends(0)
    wait_sends(1)
    for ch in range(CHUNKS):
        wait_chunk(1, ch)
    for ch in range(CHUNKS):
        composite(1, ch, image_b)


def finish(image_a, image_b, field, first, second, next_hbm, picture, sem, out_sem):
    layers = field.shape[0]
    quarter = layers // 4
    copies = [pltpu.make_async_copy(field.at[pl.ds(q * quarter, quarter)], next_hbm.at[pl.ds(q * quarter, quarter)], sem.at[q]) for q in range(4)]
    for copy in copies:
        copy.start()
    for f, (image, out) in enumerate(((image_a, first), (image_b, second))):
        width = out.shape[1]
        for c in range(out.shape[0]):
            turned = image[c].T
            groups = turned.shape[0] // width
            picture[f, c] = jnp.concatenate([turned[g * width:(g + 1) * width] for g in range(groups)], axis=1)
        copies.append(pltpu.make_async_copy(picture.at[f], out, out_sem.at[f]))
        copies[-1].start()
    for copy in copies:
        copy.wait()


def local(dims, level_set, velocity, view_flag, slab_rank):
    slabs, images, layers, rows, cols = dims
    f32 = jnp.float32
    dma = pltpu.SemaphoreType.DMA
    cells = layers * rows * cols
    level = jax.ShapeDtypeStruct((layers, rows, cols), f32)
    packed = jax.ShapeDtypeStruct((4, 8 * CHUNKS, 128), f32)
    near = pl.BlockSpec(memory_space=pltpu.VMEM)
    far = pl.BlockSpec(memory_space=pltpu.HBM)
    parts = pl.pallas_call(
        functools.partial(kernel, dims),
        out_shape=(packed, packed, level),
        in_specs=[far] * 3,
        out_specs=(near, near, near),
        scratch_shapes=[pltpu.VMEM((layers, rows, cols), f32)] * 4 + [
            pltpu.SMEM((2 * slabs,), jnp.int32),
            pltpu.VMEM((3, layers, rows, cols), f32),
            pltpu.VMEM((2, STEPS, rows, cols), f32),
            pltpu.VMEM((2, STEPS, layers, 1, cols), f32),
            pltpu.VMEM((2, STEPS, layers, 1, cols), f32),
            pltpu.VMEM((2, slabs, CHUNKS, 3, 8, 128), f32),
            pltpu.VMEM((slabs, CHUNKS, 3, 8, 128), f32),
            pltpu.VMEM((slabs, CHUNKS, 3, 8, 128), f32),
            pltpu.SMEM((slabs,), jnp.int32),
            dma((3,)),
            dma((2, STEPS)),
            dma((2, STEPS)),
            dma((2, 2, STEPS)),
            dma((2, 2, STEPS)),
            dma((2, CHUNKS, slabs)),
            dma((2, CHUNKS, slabs)),
            dma((2, CHUNKS)),
        ],
        compiler_params=pltpu.CompilerParams(collective_id=0, has_side_effects=True, vmem_limit_bytes=51 * 1024 * 1024),
        cost_estimate=pl.CostEstimate(flops=1000000 * cells, bytes_accessed=0 * cells, transcendentals=6 * cells),
    )(jnp.concatenate([view_flag, slab_rank]), level_set, velocity)
    picture = jax.ShapeDtypeStruct((4, cols // slabs, rows), f32)
    first, second, field = pl.pallas_call(
        finish,
        out_shape=(picture, picture, level),
        in_specs=[near, near, pl.BlockSpec(memory_space=pl.ANY)],
        out_specs=(far, far, far),
        scratch_shapes=[pltpu.VMEM((2, 4, cols // slabs, rows), f32), dma((4,)), dma((2,))],
        compiler_params=pltpu.CompilerParams(vmem_limit_bytes=4 * 1024 * 1024),
        cost_estimate=pl.CostEstimate(flops=cells, bytes_accessed=8 * cells, transcendentals=0),
    )(*parts)
    return (first.transpose(0, 2, 1), second.transpose(0, 2, 1), field)


def solution(mesh):
    slabs, images = mesh.shape["depth"], mesh.shape["image"]

    def whole(level_set, velocity, view_flag, slab_rank):
        layers, rows, cols = level_set.shape
        dims = (slabs, images, layers // slabs, rows // images, cols)
        placed = (P("depth", "image", None), P(None, "depth", "image", None), P(), P())
        return jax.shard_map(
            functools.partial(local, dims),
            mesh=mesh,
            in_specs=placed,
            out_specs=(P(None, "image", "depth"), P(None, "image", "depth"), P("depth", "image", None)),
            check_vma=False,
        )(level_set, velocity, view_flag, slab_rank)

    return whole
```
